32 devices in a mesh: groups: 2 (over y), dp: 4 (over z), split: 4 (over x, core).
Axes of the slice: x: 2, y: 2, z: 4, core: 2. Of those that a mesh axis runs over, the one named last changes fastest.
Arguments:
- embeddings: bfloat16 [32768, 1536], P(('groups', 'dp', 'split')), parts along dimension 0, may hold values from -144 to 144
- subcentroids: bfloat16 [8, 256, 1536], P(('groups', 'dp')), parts along dimension 0, may hold values from -16 to 16
- block_cluster: int32 [256], P(('groups', 'dp', 'split')), parts along dimension 0, may hold values from 0 to 3, as said below
- owner_map: int32 [8], P('groups'), parts along dimension 0, may hold values from 0 to 3, each once
Outputs:
- assignment: bfloat16 [32768, 256], P(('groups', 'dp', 'split')), parts along dimension 0
- centres: bfloat16 [8, 256, 1536], P(('groups', 'dp'), 'split'), parts along dimension 0
The draws below stay inside these ranges and needn't reach their ends.
There are 2 independent parts, one for each index of `groups`. The reference program is written for one: setup_inputs(seed, part) draws one part's arguments, and reference() takes and returns one part's arrays. A program takes and returns all parts, laid end to end along the dimension named above; each array names one. Nothing has to cross between parts.
Inputs may be any that keep to these rules, and one draw needn't show every extreme that they name: `block_cluster`: among the 8 blocks of one device no cluster is named more than 4 times; one cluster, the same for every device, is named exactly 4 times by every device. `owner_map`: A permutation.
All inputs are finite; a program needn't handle non-finite values.
Results may differ from the reference program's by a relative error of at most 0.008.
Values may be sent and summed in bfloat16 or wider, within the bound.
A program may use at most 128 MiB of HBM per device.

```python
import jax
import jax.numpy as jnp
from jax import lax

D = 1536
K = 256
BLOCK_ROWS = 128
ITERS = 2
BLK_DEV = 8
CAP = 4
BLOCKS = 128
TOKENS = 16384
N_DP = 4


def draw_embeddings(key, part):
    key = jax.random.fold_in(key, 11)
    values = jnp.clip(jax.random.normal(key, (TOKENS, D), jnp.float32), -6.0, 6.0)
    return values.astype(jnp.bfloat16)


def draw_subcentroids(key, part):
    key = jax.random.fold_in(key, 12)
    values = jnp.clip(0.5 * jax.random.normal(key, (N_DP, K, D), jnp.float32), -3.0, 3.0)
    return values.astype(jnp.bfloat16)


def draw_block_cluster(key, part):
    key = jax.random.fold_in(key, 13)
    hot_key, slot_key = jax.random.split(key)
    hot_cluster = jax.random.randint(hot_key, (), 0, N_DP)

    def one_device(device_key):
        shuffle_key, place_key = jax.random.split(device_key)
        shuffled = jax.random.permutation(shuffle_key, N_DP * CAP)
        clusters = shuffled // CAP
        priority = jnp.where(clusters == hot_cluster, -1, jnp.arange(N_DP * CAP))
        chosen_order = jnp.argsort(priority, stable=True)
        chosen = clusters[chosen_order[:BLK_DEV]]
        return jax.random.permutation(place_key, chosen)
    device_keys = jax.random.split(slot_key, BLOCKS // BLK_DEV)
    return jax.vmap(one_device)(device_keys).reshape(BLOCKS).astype(jnp.int32)


def setup_inputs(seed: int = 0, part: int = 0) -> dict:
    key_list = jax.random.split(jax.random.key(seed), 5)
    part_keys = jax.random.split(jax.random.fold_in(key_list[4], part), 5)
    embeddings = draw_embeddings(jax.random.fold_in(jax.random.fold_in(key_list[4], part), 71), part)
    subcentroids = draw_subcentroids(jax.random.fold_in(jax.random.fold_in(key_list[4], part), 71), part)
    block_cluster = draw_block_cluster(jax.random.fold_in(jax.random.fold_in(key_list[4], part), 71), part)
    owner_map = jax.random.permutation(part_keys[3], N_DP).astype(jnp.int32)
    return {"embeddings": embeddings, "subcentroids": subcentroids, "block_cluster": block_cluster, "owner_map": owner_map}


prior_mass = 4.0


def soft_weights(flat_rows, centre):
    inv_root = flat_rows.shape[1] ** -0.5
    dots = lax.dot_general(flat_rows, centre, (((1,), (1,)), ((), ())), preferred_element_type=jnp.float32)
    squares = jnp.sum(jnp.square(centre.astype(jnp.float32)), axis=1)
    logits = (2.0 * dots - squares[None, :]) * inv_root
    return jax.nn.softmax(logits, axis=-1).astype(jnp.bfloat16)


def renew(weighted, weight_mass, previous):
    return ((weighted + prior_mass * previous.astype(jnp.float32)) / (weight_mass[..., None] + prior_mass)).astype(jnp.bfloat16)


def reference(embeddings, subcentroids, block_cluster, owner_map):
    blocks = embeddings.reshape(BLOCKS, BLOCK_ROWS, D)
    owner_dev = owner_map[block_cluster].astype(jnp.int32)
    current = subcentroids
    weights = None
    for sweep in range(ITERS):
        def per_block(running, element, current=current):
            weighted, weight_mass = running
            rows_in, owner_now = element
            centre = lax.dynamic_index_in_dim(current, owner_now, 0, keepdims=False)
            scored = soft_weights(rows_in, centre)
            term = lax.dot_general(scored, rows_in, (((0,), (0,)), ((), ())), preferred_element_type=jnp.float32)
            weighted = weighted.at[owner_now].add(term)
            weight_mass = weight_mass.at[owner_now].add(jnp.sum(scored, axis=0, dtype=jnp.float32))
            return (weighted, weight_mass), scored

        initial = (jnp.zeros((N_DP, K, D), jnp.float32), jnp.zeros((N_DP, K), jnp.float32))
        (weighted, weight_mass), weights = lax.scan(per_block, initial, (blocks, owner_dev))
        current = renew(weighted, weight_mass, current)
    return weights.reshape(TOKENS, K), current
```

```python
import functools

import jax
import jax.numpy as jnp
from jax import lax
from jax.experimental import pallas as pl
from jax.experimental.pallas import tpu as pltpu
from jax.sharding import PartitionSpec as P

MESH = pl.DeviceIdType.MESH
ITERS = 2
PRIOR = 4.0
LANES = 128


def split_mass(mass):
    high = mass.astype(jnp.bfloat16).astype(jnp.float32)
    lane = lax.broadcasted_iota(jnp.int32, (mass.shape[0], LANES), 1)
    return jnp.where(lane < LANES // 2, high, mass - high).astype(jnp.bfloat16)


def join_mass(pair):
    return pair[:, :1] + pair[:, LANES // 2 : LANES // 2 + 1]


def kernel(
    owners, chips, cap,
    cluster_ref, owner_ref, rows_hbm, sub_hbm,
    weight_out, centre_out,
    rows, cents, wts, squares, wcat, part, from_core, from_chip, from_owner,
    load_sem, gz_send, gz_recv, gx_send, gx_recv, gc_send, gc_recv,
    rc_send, rc_recv, rx_send, rx_recv, rz_send, rz_recv,
):
    blocks, block_rows, width = rows.shape
    parts, portion = cents.shape[1], cents.shape[2]
    subs = parts * portion
    inv_root = width ** (-0.5)
    z = lax.axis_index("dp")
    s = lax.axis_index("split")
    x = lax.div(s, 2)
    c = s - 2 * x
    sibling = 2 * x + (1 - c)

    def owner_at(i):
        return lax.rem(z + i, owners)

    def chip_at(j):
        return lax.rem(x + j, chips)

    def remote(src, dst, send, recv, axis, index):
        return pltpu.make_async_remote_copy(
            src_ref=src, dst_ref=dst, send_sem=send, recv_sem=recv,
            device_id={axis: index}, device_id_type=MESH,
        )

    load_rows = pltpu.make_async_copy(rows_hbm, rows, load_sem.at[0])
    load_sub = pltpu.make_async_copy(sub_hbm, cents.at[z], load_sem.at[1])
    load_sub.start()
    load_rows.start()

    barrier = pltpu.get_barrier_semaphore()
    pl.semaphore_signal(barrier, inc=1, device_id={"split": sibling}, device_id_type=MESH)
    for j in range(1, chips):
        pl.semaphore_signal(barrier, inc=1, device_id={"split": 2 * chip_at(j) + c}, device_id_type=MESH)
    for i in range(1, owners):
        pl.semaphore_signal(barrier, inc=1, device_id={"dp": owner_at(i)}, device_id_type=MESH)
    pl.semaphore_wait(barrier, 1 + (chips - 1) + (owners - 1))
    load_sub.wait()

    def gz(i):
        ref = cents.at[z, s]
        return remote(ref, ref, gz_send.at[i], gz_recv.at[z], "dp", lax.rem(z + owners - i, owners))

    def gz_from(o):
        ref = cents.at[o, s]
        return remote(ref, ref, gz_send.at[0], gz_recv.at[o], "dp", owner_at(1))

    def gx(o, j):
        ref = cents.at[o, s]
        return remote(ref, ref, gx_send.at[o, j], gx_recv.at[o, x], "split", 2 * chip_at(j) + c)

    def gx_from(o, j):
        ref = cents.at[o, 2 * chip_at(j) + c]
        return remote(ref, ref, gx_send.at[o, j], gx_recv.at[o, chip_at(j)], "split", 2 * chip_at(j) + c)

    def gc(o, chip):
        ref = cents.at[o, 2 * chip + c]
        return remote(ref, ref, gc_send.at[o, chip], gc_recv.at[o, chip], "split", sibling)

    def gc_from(o, chip):
        ref = cents.at[o, 2 * chip + 1 - c]
        return remote(ref, ref, gc_send.at[o, chip], gc_recv.at[o, chip], "split", sibling)

    def gather(first):
        for i in range(1, owners):
            gz(i).start()

        @pl.loop(first, owners)
        def _(i):
            o = owner_at(i)

            @pl.when(i > 0)
            def _():
                gz_from(o).wait_recv()

            for j in range(1, chips):
                gx(o, j).start()
            gc(o, x).start()

        @pl.loop(first, owners)
        def _(i):
            o = owner_at(i)
            for j in range(1, chips):
                gx_from(o, j).wait_recv()
                gc(o, chip_at(j)).start()

        @pl.loop(first, owners)
        def _(i):
            o = owner_at(i)
            for chip in range(chips):
                gc_from(o, chip).wait_recv()
                gc(o, chip).wait_send()
            for j in range(1, chips):
                gx(o, j).wait_send()

        for i in range(1, owners):
            gz(i).wait_send()

    def score(last):
        @pl.loop(0, owners)
        def _(o):
            held = cents[o].reshape(subs, width).astype(jnp.float32)
            squares[o] = jnp.sum(held * held, axis=1, keepdims=True)

        @pl.loop(0, blocks)
        def _(b):
            o = owner_ref[cluster_ref[b]]
            centre = cents[o].reshape(subs, width)
            dots = lax.dot_general(
                centre, rows[b], (((1,), (1,)), ((), ())), preferred_element_type=jnp.float32
            )
            logits = (2.0 * dots - squares[o]) * inv_root
            power = jnp.exp(logits - jnp.max(logits, axis=0, keepdims=True))
            weight = power / jnp.sum(power, axis=0, keepdims=True)
            wts[b] = weight.astype(jnp.bfloat16)
            if last:
                weight_out[b] = weight.T.astype(jnp.bfloat16)

    def rc(o):
        return remote(part.at[o, 1 - c], from_core.at[o], rc_send.at[o], rc_recv.at[o], "split", sibling)

    def rx(o, j):
        return remote(
            part.at[o, c, chip_at(j)], from_chip.at[o, j - 1], rx_send.at[o, j], rx_recv.at[o, j],
            "split", 2 * chip_at(j) + c,
        )

    def rx_from(o, j):
        return remote(
            part.at[o, c, x], from_chip.at[o, j - 1], rx_send.at[o, j], rx_recv.at[o, j],
            "split", 2 * chip_at(j) + c,
        )

    def rz(o):
        return remote(part.at[o, c, x], from_owner.at[z], rz_send.at[o], rz_recv.at[z], "dp", o)

    def rz_from(o):
        return remote(part.at[o, c, x], from_owner.at[o], rz_send.at[o], rz_recv.at[o], "dp", o)

    def weigh(o):
        ids = [jnp.int32(0)] * cap
        live = [jnp.int32(0)] * cap
        count = jnp.int32(0)
        for b in range(blocks):
            hit = jnp.where(owner_ref[cluster_ref[b]] == o, jnp.int32(1), jnp.int32(0))
            for j in range(cap):
                take = hit * jnp.where(count == j, jnp.int32(1), jnp.int32(0))
                ids[j] = ids[j] + take * b
                live[j] = live[j] + take
            count = count + hit
        mass = jnp.zeros((subs, 1), jnp.float32)
        for j in range(cap):
            piece = wts[ids[j]].astype(jnp.float32) * live[j].astype(jnp.float32)
            wcat[:, j * block_rows : (j + 1) * block_rows] = piece.astype(jnp.bfloat16)
            mass = mass + jnp.sum(piece, axis=1, keepdims=True)
        mass = split_mass(mass)
        step = 512 if width % 512 == 0 else width
        weights = wcat[...]
        for n in range(width // step):
            cols = slice(n * step, (n + 1) * step)
            taken = jnp.concatenate([rows[ids[j], :, cols] for j in range(cap)], axis=0)
            sums = jnp.dot(weights, taken, preferred_element_type=jnp.float32).astype(jnp.bfloat16)
            for q in range(parts):
                part[o, q % 2, q // 2, :, cols] = sums[q * portion : (q + 1) * portion]
        for q in range(parts):
            part[o, q % 2, q // 2, :, width:] = mass[q * portion : (q + 1) * portion]

    def store_sum(o, chip, total):
        part[o, c, chip, :, :width] = total[:, :width].astype(jnp.bfloat16)
        part[o, c, chip, :, width:] = split_mass(join_mass(total[:, width:]))

    def reduce(last):
        @pl.loop(0, owners + 2)
        def _(t):
            @pl.when(t < owners)
            def _():
                o = owner_at(1 + t)
                weigh(o)
                rc(o).start()

            @pl.when((t >= 1) & (t <= owners))
            def _():
                o = owner_at(t)
                rc(o).wait_recv()
                for j in range(1, chips + 1):
                    chip = chip_at(j)
                    store_sum(o, chip, part[o, c, chip].astype(jnp.float32) + from_core[o, chip].astype(jnp.float32))
                    if j < chips:
                        rx(o, j).start()

            @pl.when(t >= 2)
            def _():
                o = owner_at(t - 1)
                total = part[o, c, x].astype(jnp.float32)
                for j in range(1, chips):
                    rx_from(o, j).wait_recv()
                    total = total + from_chip[o, j - 1].astype(jnp.float32)
                store_sum(o, x, total)

                @pl.when(t < owners + 1)
                def _():
                    rz(o).start()

        total = part[z, c, x].astype(jnp.float32)
        for i in range(1, owners):
            o = owner_at(owners - i)
            rz_from(o).wait_recv()
            total = total + from_owner[o].astype(jnp.float32)
        mass = join_mass(total[:, width:])
        renewed = (total[:, :width] + PRIOR * cents[z, s].astype(jnp.float32)) / (mass + PRIOR)
        if last:
            centre_out[...] = renewed.astype(jnp.bfloat16)
        else:
            cents[z, s] = renewed.astype(jnp.bfloat16)

    def reduce_done():
        @pl.loop(0, owners)
        def _(t):
            o = owner_at(1 + t)
            rc(o).wait_send()
            for j in range(1, chips):
                rx(o, j).wait_send()

            @pl.when(t < owners - 1)
            def _():
                rz(o).wait_send()

    for sweep in range(ITERS):
        gather(1 if sweep == 0 else 0)
        if sweep == 0:
            load_rows.wait()
        else:
            reduce_done()
        score(sweep == ITERS - 1)
        reduce(sweep == ITERS - 1)
    reduce_done()


def body(embeddings, subcentroids, block_cluster, owner_map):
    owners = lax.axis_size("dp")
    parts = lax.axis_size("split")
    chips = parts // 2
    blocks = block_cluster.shape[0]
    total_rows, width = embeddings.shape
    block_rows = total_rows // blocks
    cap = max(2, 2 * blocks // owners)
    subs = subcentroids.shape[1]
    portion = subs // parts
    wide = width + LANES
    bf16 = jnp.bfloat16
    sems = pltpu.SemaphoreType.DMA
    flops = 2 * ITERS * subs * width * block_rows * (blocks + owners * cap)
    weights, centres = pl.pallas_call(
        functools.partial(kernel, owners, chips, cap),
        out_shape=(
            jax.ShapeDtypeStruct((blocks, block_rows, subs), bf16),
            jax.ShapeDtypeStruct((portion, width), bf16),
        ),
        in_specs=[
            pl.BlockSpec(memory_space=pltpu.SMEM),
            pl.BlockSpec(memory_space=pltpu.SMEM),
            pl.BlockSpec(memory_space=pl.ANY),
            pl.BlockSpec(memory_space=pl.ANY),
        ],
        out_specs=(
            pl.BlockSpec(memory_space=pltpu.VMEM),
            pl.BlockSpec(memory_space=pltpu.VMEM),
        ),
        scratch_shapes=[
            pltpu.VMEM((blocks, block_rows, width), bf16),
            pltpu.VMEM((owners, parts, portion, width), bf16),
            pltpu.VMEM((blocks, subs, block_rows), bf16),
            pltpu.VMEM((owners, subs, 1), jnp.float32),
            pltpu.VMEM((subs, cap * block_rows), bf16),
            pltpu.VMEM((owners, 2, chips, portion, wide), bf16),
            pltpu.VMEM((owners, chips, portion, wide), bf16),
            pltpu.VMEM((owners, max(1, chips - 1), portion, wide), bf16),
            pltpu.VMEM((owners, portion, wide), bf16),
            sems((2,)),
            sems((owners,)), sems((owners,)),
            sems((owners, chips)), sems((owners, chips)),
            sems((owners, chips)), sems((owners, chips)),
            sems((owners,)), sems((owners,)),
            sems((owners, chips)), sems((owners, chips)),
            sems((owners,)), sems((owners,)),
        ],
        compiler_params=pltpu.CompilerParams(
            collective_id=0, has_side_effects=True, vmem_limit_bytes=58 * 1024 * 1024
        ),
        cost_estimate=pl.CostEstimate(
            flops=flops, bytes_accessed=2 * total_rows * width, transcendentals=total_rows * subs
        ),
    )(
        block_cluster, owner_map,
        embeddings.reshape(blocks, block_rows, width),
        subcentroids.reshape(parts, portion, width),
    )
    return weights.reshape(total_rows, subs), centres[None]


def solution(mesh):
    return jax.shard_map(
        body,
        mesh=mesh,
        in_specs=(
            P(("groups", "dp", "split"), None),
            P(("groups", "dp"), None, None),
            P(("groups", "dp", "split")),
            P("groups"),
        ),
        out_specs=(P(("groups", "dp", "split"), None), P(("groups", "dp"), "split", None)),
        check_vma=False,
    )
```

```python
import functools

import jax
import jax.numpy as jnp
from jax import lax
from jax.experimental import pallas as pl
from jax.experimental.pallas import tpu as pltpu
from jax.sharding import PartitionSpec as P

MESH = pl.DeviceIdType.MESH
ITERS = 2
PRIOR = 4.0
LANES = 128
LAG = 4


def split_mass(mass):
    high = mass.astype(jnp.bfloat16).astype(jnp.float32)
    lane = lax.broadcasted_iota(jnp.int32, (mass.shape[0], LANES), 1)
    return jnp.where(lane < LANES // 2, high, mass - high).astype(jnp.bfloat16)


def join_mass(pair):
    return pair[:, :1] + pair[:, LANES // 2 : LANES // 2 + 1]


def kernel(
    owners, chips, cap,
    cluster_ref, owner_ref, rows_hbm, sub_hbm,
    weight_out, centre_out,
    rows, cents, wts, squares, wcat, part, from_core, from_chip, from_owner, sums,
    load_sem, gz_send, gz_recv, gx_send, gx_recv, gc_send, gc_recv,
    rc_send, rc_recv, rx_send, rx_recv, rz_send, rz_recv,
):
    blocks, block_rows, width = rows.shape
    parts, portion = cents.shape[1], cents.shape[2]
    subs = parts * portion
    inv_root = width ** (-0.5)
    z = lax.axis_index("dp")
    s = lax.axis_index("split")
    x = lax.div(s, 2)
    c = s - 2 * x
    sibling = 2 * x + (1 - c)
    halves = 2 if portion % 32 == 0 else 1
    rows_half = portion // halves

    def span(h):
        return pl.ds(pl.multiple_of(h * rows_half, rows_half), rows_half)

    def chip_at(j):
        return lax.rem(x + j, chips)

    def remote(src, dst, send, recv, axis, index):
        return pltpu.make_async_remote_copy(
            src_ref=src, dst_ref=dst, send_sem=send, recv_sem=recv,
            device_id={axis: index}, device_id_type=MESH,
        )

    load_rows = pltpu.make_async_copy(rows_hbm, rows, load_sem.at[0])
    load_sub = pltpu.make_async_copy(sub_hbm, cents.at[z], load_sem.at[1])
    load_sub.start()
    load_rows.start()

    barrier = pltpu.get_barrier_semaphore()
    pl.semaphore_signal(barrier, inc=1, device_id={"split": sibling}, device_id_type=MESH)
    for j in range(1, chips):
        pl.semaphore_signal(barrier, inc=1, device_id={"split": 2 * chip_at(j) + c}, device_id_type=MESH)
    for way in range(2):

        @pl.when(z < owners - 1 if way == 0 else z > 0)
        def _():
            pl.semaphore_signal(barrier, inc=1, device_id={"dp": z + 1 - 2 * way}, device_id_type=MESH)

    links = jnp.where(z > 0, 1, 0) + jnp.where(z < owners - 1, 1, 0)
    pl.semaphore_wait(barrier, chips + links)
    load_sub.wait()

    def gz(o, h, way):
        ref = cents.at[o, s, span(h)]
        return remote(ref, ref, gz_send.at[o, h, way], gz_recv.at[o, h], "dp", z + 1 - 2 * way)

    def gz_from(o, h, way):
        ref = cents.at[o, s, span(h)]
        return remote(ref, ref, gz_send.at[o, h, way], gz_recv.at[o, h], "dp", z - 1 + 2 * way)

    def has_next(way):
        return z < owners - 1 if way == 0 else z > 0

    def gx(o, h, j):
        ref = cents.at[o, s, span(h)]
        return remote(ref, ref, gx_send.at[o, h, j], gx_recv.at[o, h, x], "split", 2 * chip_at(j) + c)

    def gx_from(o, h, j):
        ref = cents.at[o, 2 * chip_at(j) + c, span(h)]
        return remote(ref, ref, gx_send.at[o, h, j], gx_recv.at[o, h, chip_at(j)], "split", 2 * chip_at(j) + c)

    def gc(o, h, chip):
        ref = cents.at[o, 2 * chip + c, span(h)]
        return remote(ref, ref, gc_send.at[o, h, chip], gc_recv.at[o, h, chip], "split", sibling)

    def gc_from(o, h, chip):
        ref = cents.at[o, 2 * chip + 1 - c, span(h)]
        return remote(ref, ref, gc_send.at[o, h, chip], gc_recv.at[o, h, chip], "split", sibling)

    def spread(o, h):
        for j in range(1, chips):
            gx(o, h, j).start()
        gc(o, h, x).start()

    def pass_on(o, h):
        for j in range(1, chips):
            gx_from(o, h, j).wait_recv()
            gc(o, h, chip_at(j)).start()

    def settle(o):
        for h in range(halves):
            for chip in range(chips):
                gc_from(o, h, chip).wait_recv()
                gc(o, h, chip).wait_send()
            for j in range(1, chips):
                gx(o, h, j).wait_send()

    def at_distance(k, act):
        for way in range(2):
            o = z - k if way == 0 else z + k

            @pl.when(o >= 0 if way == 0 else o < owners)
            def _():
                act(o, way)

    def onward(o, h, way, done):
        @pl.when(has_next(way))
        def _():
            if done:
                gz(o, h, way).wait_send()
            else:
                gz(o, h, way).start()

    def gather(first):
        for h in range(halves):
            for way in range(2):
                onward(z, h, way, False)
            if not first:
                spread(z, h)

        @pl.loop(1, owners + 1)
        def _(k):
            for h in range(halves):

                def arrive(o, way, h=h):
                    gz_from(o, h, way).wait_recv()
                    onward(o, h, way, False)
                    spread(o, h)

                at_distance(k, arrive)

                @pl.when(k > 1)
                def _():
                    at_distance(k - 1, lambda o, way, h=h: pass_on(o, h))

                if not first:

                    @pl.when(k == 1)
                    def _():
                        pass_on(z, h)

        def finish(o, way):
            for h in range(halves):
                onward(o, h, way, True)
            settle(o)

        for h in range(halves):
            for way in range(2):
                onward(z, h, way, True)
        if not first:
            settle(z)

        @pl.loop(1, owners)
        def _(k):
            at_distance(k, finish)

    def score(last):
        @pl.loop(0, owners)
        def _(o):
            held = cents[o].reshape(subs, width).astype(jnp.float32)
            squares[o] = jnp.sum(held * held, axis=1, keepdims=True)

        @pl.loop(0, blocks)
        def _(b):
            o = owner_ref[cluster_ref[b]]
            centre = cents[o].reshape(subs, width)
            dots = lax.dot_general(
                centre, rows[b], (((1,), (1,)), ((), ())), preferred_element_type=jnp.float32
            )
            logits = (2.0 * dots - squares[o]) * inv_root
            power = jnp.exp(logits - jnp.max(logits, axis=0, keepdims=True))
            weight = power / jnp.sum(power, axis=0, keepdims=True)
            wts[b] = weight.astype(jnp.bfloat16)
            if last:
                weight_out[b] = weight.T.astype(jnp.bfloat16)

    def rc(o):
        return remote(part.at[o, 1 - c], from_core.at[o], rc_send.at[o], rc_recv.at[o], "split", sibling)

    def rx(o, h, j):
        return remote(
            part.at[o, c, chip_at(j), span(h)], from_chip.at[o, j - 1, span(h)],
            rx_send.at[o, h, j], rx_recv.at[o, h, j], "split", 2 * chip_at(j) + c,
        )

    def rz(o, h, way):
        slot = o if way == 0 else jnp.where(o == z - 1, owners, o)
        return remote(
            part.at[o, c, x, span(h)], from_owner.at[slot, span(h)],
            rz_send.at[o, h], rz_recv.at[slot, h], "dp", z + 1 - 2 * way,
        )

    def rz_from(o, h, way):
        slot = o if way == 0 else jnp.where(o == z, owners, o)
        return slot, remote(
            part.at[o, c, x, span(h)], from_owner.at[slot, span(h)],
            rz_send.at[o, h], rz_recv.at[slot, h], "dp", z - 1 + 2 * way,
        )

    below, above = z, owners - 1 - z
    far = jnp.maximum(below, above)
    near = jnp.minimum(below, above)
    far_sign = jnp.where(above >= below, 1, -1)

    def farthest(t):
        u = t - (far - near)
        half = lax.div(jnp.maximum(u, 0), 2)
        sign = jnp.where(u - 2 * half == 1, -far_sign, far_sign)
        return jnp.where(u < 0, z + far_sign * (far - t), z + sign * (near - half))

    def weigh(o):
        ids = [jnp.int32(0)] * cap
        live = [jnp.int32(0)] * cap
        count = jnp.int32(0)
        for b in range(blocks):
            hit = jnp.where(owner_ref[cluster_ref[b]] == o, jnp.int32(1), jnp.int32(0))
            for j in range(cap):
                take = hit * jnp.where(count == j, jnp.int32(1), jnp.int32(0))
                ids[j] = ids[j] + take * b
                live[j] = live[j] + take
            count = count + hit
        mass = jnp.zeros((subs, 1), jnp.float32)
        for j in range(cap):
            piece = wts[ids[j]].astype(jnp.float32) * live[j].astype(jnp.float32)
            wcat[:, j * block_rows : (j + 1) * block_rows] = piece.astype(jnp.bfloat16)
            mass = mass + jnp.sum(piece, axis=1, keepdims=True)
        mass = split_mass(mass)
        step = 512 if width % 512 == 0 else width
        weights = wcat[...]
        for n in range(width // step):
            cols = slice(n * step, (n + 1) * step)
            taken = jnp.concatenate([rows[ids[j], :, cols] for j in range(cap)], axis=0)
            product = jnp.dot(weights, taken, preferred_element_type=jnp.float32).astype(jnp.bfloat16)
            for q in range(parts):
                part[o, q % 2, q // 2, :, cols] = product[q * portion : (q + 1) * portion]
        for q in range(parts):
            part[o, q % 2, q // 2, :, width:] = mass[q * portion : (q + 1) * portion]

    def store_sum(o, chip, h, total):
        part[o, c, chip, span(h), :width] = total[:, :width].astype(jnp.bfloat16)
        part[o, c, chip, span(h), width:] = split_mass(join_mass(total[:, width:]))

    def over_chips(o, h):
        total = part[o, c, x, span(h)].astype(jnp.float32)
        for j in range(1, chips):
            rx(o, h, chips - j).wait_recv()
            total = total + from_chip[o, chips - j - 1, span(h)].astype(jnp.float32)
        return total

    def reduce(last):
        units = owners * halves

        def unit(u):
            t = lax.div(u, halves)
            return farthest(t), u - t * halves

        @pl.loop(0, units + 1)
        def _(u):
            o, h = unit(u)

            @pl.when((u < units) & (h == 0))
            def _():
                weigh(o)
                rc(o).start()

            before, hb = unit(jnp.maximum(u - 1, 0))

            @pl.when(u >= 1)
            def _():
                @pl.when(hb == 0)
                def _():
                    rc(before).wait_recv()

                for j in range(1, chips + 1):
                    chip = chip_at(j)
                    store_sum(
                        before, chip, hb,
                        part[before, c, chip, span(hb)].astype(jnp.float32)
                        + from_core[before, chip, span(hb)].astype(jnp.float32),
                    )
                    if j < chips:
                        rx(before, hb, j).start()

            @pl.when(u >= LAG)
            def _():
                forward(*unit(jnp.maximum(u - LAG, 0)))

        for u in range(units + 1 - LAG, units):
            forward(*unit(u))
        for h in range(halves):
            sums[...] = over_chips(z, h)
            for way in range(2):

                @pl.when(z > 0 if way == 0 else z < owners - 1)
                def _():
                    slot, copy = rz_from(z, h, way)
                    copy.wait_recv()
                    sums[...] += from_owner[slot, span(h)].astype(jnp.float32)

            mass = join_mass(sums[:, width:])
            renewed = (sums[:, :width] + PRIOR * cents[z, s, span(h)].astype(jnp.float32)) / (mass + PRIOR)
            if last:
                centre_out[span(h)] = renewed.astype(jnp.bfloat16)
            else:
                cents[z, s, span(h)] = renewed.astype(jnp.bfloat16)

    def forward(o, h):
        for way in range(2):

            @pl.when(o > z if way == 0 else o < z)
            def _():
                total = over_chips(o, h)
                store_sum(o, x, h, total)

                @pl.when(z > 0 if way == 0 else z < owners - 1)
                def _():
                    slot, copy = rz_from(o, h, way)
                    copy.wait_recv()
                    store_sum(o, x, h, total + from_owner[slot, span(h)].astype(jnp.float32))

                rz(o, h, way).start()

    def reduce_done():
        @pl.loop(0, owners)
        def _(o):
            rc(o).wait_send()
            for h in range(halves):
                for j in range(1, chips):
                    rx(o, h, j).wait_send()

                @pl.when(o > z)
                def _():
                    rz(o, h, 0).wait_send()

                @pl.when(o < z)
                def _():
                    rz(o, h, 1).wait_send()

    for sweep in range(ITERS):
        gather(sweep == 0)
        if sweep == 0:
            load_rows.wait()
        else:
            reduce_done()
        score(sweep == ITERS - 1)
        reduce(sweep == ITERS - 1)
    reduce_done()


def body(embeddings, subcentroids, block_cluster, owner_map):
    owners = lax.axis_size("dp")
    parts = lax.axis_size("split")
    chips = parts // 2
    blocks = block_cluster.shape[0]
    total_rows, width = embeddings.shape
    block_rows = total_rows // blocks
    cap = max(2, 2 * blocks // owners)
    subs = subcentroids.shape[1]
    portion = subs // parts
    wide = width + LANES
    bf16 = jnp.bfloat16
    sems = pltpu.SemaphoreType.DMA
    flops = 2 * ITERS * subs * width * block_rows * (blocks + owners * cap)
    weights, centres = pl.pallas_call(
        functools.partial(kernel, owners, chips, cap),
        out_shape=(
            jax.ShapeDtypeStruct((blocks, block_rows, subs), bf16),
            jax.ShapeDtypeStruct((portion, width), bf16),
        ),
        in_specs=[
            pl.BlockSpec(memory_space=pltpu.SMEM),
            pl.BlockSpec(memory_space=pltpu.SMEM),
            pl.BlockSpec(memory_space=pl.ANY),
            pl.BlockSpec(memory_space=pl.ANY),
        ],
        out_specs=(
            pl.BlockSpec(memory_space=pltpu.VMEM),
            pl.BlockSpec(memory_space=pltpu.VMEM),
        ),
        scratch_shapes=[
            pltpu.VMEM((blocks, block_rows, width), bf16),
            pltpu.VMEM((owners, parts, portion, width), bf16),
            pltpu.VMEM((blocks, subs, block_rows), bf16),
            pltpu.VMEM((owners, subs, 1), jnp.float32),
            pltpu.VMEM((subs, cap * block_rows), bf16),
            pltpu.VMEM((owners, 2, chips, portion, wide), bf16),
            pltpu.VMEM((owners, chips, portion, wide), bf16),
            pltpu.VMEM((owners, max(1, chips - 1), portion, wide), bf16),
            pltpu.VMEM((owners + 1, portion, wide), bf16),
            pltpu.VMEM((portion // (2 if portion % 32 == 0 else 1), wide), jnp.float32),
            sems((2,)),
            sems((owners, 2, 2)), sems((owners, 2)),
            sems((owners, 2, chips)), sems((owners, 2, chips)),
            sems((owners, 2, chips)), sems((owners, 2, chips)),
            sems((owners,)), sems((owners,)),
            sems((owners, 2, chips)), sems((owners, 2, chips)),
            sems((owners, 2)), sems((owners + 1, 2)),
        ],
        compiler_params=pltpu.CompilerParams(
            collective_id=0, has_side_effects=True, vmem_limit_bytes=58 * 1024 * 1024
        ),
        cost_estimate=pl.CostEstimate(
            flops=flops, bytes_accessed=2 * total_rows * width, transcendentals=total_rows * subs
        ),
    )(
        block_cluster, owner_map,
        embeddings.reshape(blocks, block_rows, width),
        subcentroids.reshape(parts, portion, width),
    )
    return weights.reshape(total_rows, subs), centres[None]


def solution(mesh):
    return jax.shard_map(
        body,
        mesh=mesh,
        in_specs=(
            P(("groups", "dp", "split"), None),
            P(("groups", "dp"), None, None),
            P(("groups", "dp", "split")),
            P("groups"),
        ),
        out_specs=(P(("groups", "dp", "split"), None), P(("groups", "dp"), "split", None)),
        check_vma=False,
    )
```

```python
import functools

import jax
import jax.numpy as jnp
from jax import lax
from jax.experimental import pallas as pl
from jax.experimental.pallas import tpu as pltpu
from jax.sharding import PartitionSpec as P

MESH = pl.DeviceIdType.MESH
ITERS = 2
PRIOR = 4.0
LANES = 128
LAG = 4


def split_mass(mass):
    high = mass.astype(jnp.bfloat16).astype(jnp.float32)
    lane = lax.broadcasted_iota(jnp.int32, (mass.shape[0], LANES), 1)
    return jnp.where(lane < LANES // 2, high, mass - high).astype(jnp.bfloat16)


def join_mass(pair):
    return pair[:, :1] + pair[:, LANES // 2 : LANES // 2 + 1]


def kernel(
    owners, chips, cap,
    cluster_ref, owner_ref, rows_hbm, sub_hbm,
    weight_out, centre_out,
    rows, cents, wts, wcat, part, from_core, from_chip, from_owner, sums,
    load_sem, gz_send, gz_recv, gx_send, gx_recv, gc_send, gc_recv,
    rc_send, rc_recv, rx_send, rx_recv, rz_send, rz_recv,
):
    blocks, block_rows, width = rows.shape
    parts, portion = cents.shape[1], cents.shape[2]
    subs = parts * portion
    inv_root = width ** (-0.5)
    z = lax.axis_index("dp")
    s = lax.axis_index("split")
    x = lax.div(s, 2)
    c = s - 2 * x
    sibling = 2 * x + (1 - c)
    halves = 2 if portion % 32 == 0 else 1
    rows_half = portion // halves

    def span(h):
        return pl.ds(pl.multiple_of(h * rows_half, rows_half), rows_half)

    def chip_at(j):
        return lax.rem(x + j, chips)

    def remote(src, dst, send, recv, axis, index):
        return pltpu.make_async_remote_copy(
            src_ref=src, dst_ref=dst, send_sem=send, recv_sem=recv,
            device_id={axis: index}, device_id_type=MESH,
        )

    load_rows = pltpu.make_async_copy(rows_hbm, rows, load_sem.at[0])
    load_sub = pltpu.make_async_copy(sub_hbm, cents.at[z], load_sem.at[1])
    load_sub.start()
    load_rows.start()

    barrier = pltpu.get_barrier_semaphore()
    pl.semaphore_signal(barrier, inc=1, device_id={"split": sibling}, device_id_type=MESH)
    for j in range(1, chips):
        pl.semaphore_signal(barrier, inc=1, device_id={"split": 2 * chip_at(j) + c}, device_id_type=MESH)
    for way in range(2):

        @pl.when(z < owners - 1 if way == 0 else z > 0)
        def _():
            pl.semaphore_signal(barrier, inc=1, device_id={"dp": z + 1 - 2 * way}, device_id_type=MESH)

    links = jnp.where(z > 0, 1, 0) + jnp.where(z < owners - 1, 1, 0)
    pl.semaphore_wait(barrier, chips + links)
    load_sub.wait()

    def gz(o, h, way):
        ref = cents.at[o, s, span(h)]
        return remote(ref, ref, gz_send.at[o, h, way], gz_recv.at[o, h], "dp", z + 1 - 2 * way)

    def gz_from(o, h, way):
        ref = cents.at[o, s, span(h)]
        return remote(ref, ref, gz_send.at[o, h, way], gz_recv.at[o, h], "dp", z - 1 + 2 * way)

    def has_next(way):
        return z < owners - 1 if way == 0 else z > 0

    def gx(o, h, j):
        ref = cents.at[o, s, span(h)]
        return remote(ref, ref, gx_send.at[o, h, j], gx_recv.at[o, h, x], "split", 2 * chip_at(j) + c)

    def gx_from(o, h, j):
        ref = cents.at[o, 2 * chip_at(j) + c, span(h)]
        return remote(ref, ref, gx_send.at[o, h, j], gx_recv.at[o, h, chip_at(j)], "split", 2 * chip_at(j) + c)

    def gc(o, h, chip):
        ref = cents.at[o, 2 * chip + c, span(h)]
        return remote(ref, ref, gc_send.at[o, h, chip], gc_recv.at[o, h, chip], "split", sibling)

    def gc_from(o, h, chip):
        ref = cents.at[o, 2 * chip + 1 - c, span(h)]
        return remote(ref, ref, gc_send.at[o, h, chip], gc_recv.at[o, h, chip], "split", sibling)

    def spread(o, h):
        for j in range(1, chips):
            gx(o, h, j).start()
        gc(o, h, x).start()

    def pass_on(o, h):
        for j in range(1, chips):
            gx_from(o, h, j).wait_recv()
            gc(o, h, chip_at(j)).start()

    def settle(o):
        for h in range(halves):
            for chip in range(chips):
                gc_from(o, h, chip).wait_recv()
                gc(o, h, chip).wait_send()
            for j in range(1, chips):
                gx(o, h, j).wait_send()

    def at_distance(k, act):
        for way in range(2):
            o = z - k if way == 0 else z + k

            @pl.when(o >= 0 if way == 0 else o < owners)
            def _():
                act(o, way)

    def onward(o, h, way, done):
        @pl.when(has_next(way))
        def _():
            if done:
                gz(o, h, way).wait_send()
            else:
                gz(o, h, way).start()

    def gather(first):
        for h in range(halves):
            for way in range(2):
                onward(z, h, way, False)
            if not first:
                spread(z, h)

        @pl.loop(1, owners + 1)
        def _(k):
            for h in range(halves):

                def arrive(o, way, h=h):
                    gz_from(o, h, way).wait_recv()
                    onward(o, h, way, False)
                    spread(o, h)

                at_distance(k, arrive)

                @pl.when(k > 1)
                def _():
                    at_distance(k - 1, lambda o, way, h=h: pass_on(o, h))

                if not first:

                    @pl.when(k == 1)
                    def _():
                        pass_on(z, h)

        def finish(o, way):
            for h in range(halves):
                onward(o, h, way, True)
            settle(o)

        for h in range(halves):
            for way in range(2):
                onward(z, h, way, True)
        if not first:
            settle(z)

        @pl.loop(1, owners)
        def _(k):
            at_distance(k, finish)

    def rc(o):
        return remote(part.at[o, 1 - c], from_core.at[o], rc_send.at[o], rc_recv.at[o], "split", sibling)

    def rx(o, h, j):
        return remote(
            part.at[o, c, chip_at(j), span(h)], from_chip.at[o, j - 1, span(h)],
            rx_send.at[o, h, j], rx_recv.at[o, h, j], "split", 2 * chip_at(j) + c,
        )

    def rz(o, h, way):
        slot = o if way == 0 else jnp.where(o == z - 1, owners, o)
        return remote(
            part.at[o, c, x, span(h)], from_owner.at[slot, span(h)],
            rz_send.at[o, h], rz_recv.at[slot, h], "dp", z + 1 - 2 * way,
        )

    def rz_from(o, h, way):
        slot = o if way == 0 else jnp.where(o == z, owners, o)
        return slot, remote(
            part.at[o, c, x, span(h)], from_owner.at[slot, span(h)],
            rz_send.at[o, h], rz_recv.at[slot, h], "dp", z - 1 + 2 * way,
        )

    below, above = z, owners - 1 - z
    far = jnp.maximum(below, above)
    near = jnp.minimum(below, above)
    far_sign = jnp.where(above >= below, 1, -1)

    def farthest(t):
        u = t - (far - near)
        half = lax.div(jnp.maximum(u, 0), 2)
        sign = jnp.where(u - 2 * half == 1, -far_sign, far_sign)
        return jnp.where(u < 0, z + far_sign * (far - t), z + sign * (near - half))

    def weigh(o, last):
        ids = [jnp.int32(0)] * cap
        live = [jnp.int32(0)] * cap
        count = jnp.int32(0)
        for b in range(blocks):
            hit = jnp.where(owner_ref[cluster_ref[b]] == o, jnp.int32(1), jnp.int32(0))
            for j in range(cap):
                take = hit * jnp.where(count == j, jnp.int32(1), jnp.int32(0))
                ids[j] = ids[j] + take * b
                live[j] = live[j] + take
            count = count + hit
        centre = cents[o].reshape(subs, width)
        held = centre.astype(jnp.float32)
        squares = jnp.sum(held * held, axis=1, keepdims=True)
        mass = jnp.zeros((subs, 1), jnp.float32)
        for j in range(cap):
            dots = lax.dot_general(
                centre, rows[ids[j]], (((1,), (1,)), ((), ())), preferred_element_type=jnp.float32
            )
            logits = (2.0 * dots - squares) * inv_root
            power = jnp.exp(logits - jnp.max(logits, axis=0, keepdims=True))
            weight = (power / jnp.sum(power, axis=0, keepdims=True)).astype(jnp.bfloat16)
            if last:
                wts[o * cap + j] = weight
            piece = weight.astype(jnp.float32) * live[j].astype(jnp.float32)
            wcat[:, j * block_rows : (j + 1) * block_rows] = piece.astype(jnp.bfloat16)
            mass = mass + jnp.sum(piece, axis=1, keepdims=True)
        mass = split_mass(mass)
        step = 512 if width % 512 == 0 else width
        weights = wcat[...]
        for n in range(width // step):
            cols = slice(n * step, (n + 1) * step)
            taken = jnp.concatenate([rows[ids[j], :, cols] for j in range(cap)], axis=0)
            product = jnp.dot(weights, taken, preferred_element_type=jnp.float32).astype(jnp.bfloat16)
            for q in range(parts):
                part[o, q % 2, q // 2, :, cols] = product[q * portion : (q + 1) * portion]
        for q in range(parts):
            part[o, q % 2, q // 2, :, width:] = mass[q * portion : (q + 1) * portion]

    def store_sum(o, chip, h, total):
        part[o, c, chip, span(h), :width] = total[:, :width].astype(jnp.bfloat16)
        part[o, c, chip, span(h), width:] = split_mass(join_mass(total[:, width:]))

    def over_chips(o, h):
        total = part[o, c, x, span(h)].astype(jnp.float32)
        for j in range(1, chips):
            rx(o, h, chips - j).wait_recv()
            total = total + from_chip[o, chips - j - 1, span(h)].astype(jnp.float32)
        return total

    def reduce(last):
        units = owners * halves

        def unit(u):
            t = lax.div(u, halves)
            return farthest(t), u - t * halves

        @pl.loop(0, units + 1)
        def _(u):
            o, h = unit(u)

            @pl.when((u < units) & (h == 0))
            def _():
                weigh(o, last)
                rc(o).start()

            before, hb = unit(jnp.maximum(u - 1, 0))

            @pl.when(u >= 1)
            def _():
                @pl.when(hb == 0)
                def _():
                    rc(before).wait_recv()

                for j in range(1, chips + 1):
                    chip = chip_at(j)
                    store_sum(
                        before, chip, hb,
                        part[before, c, chip, span(hb)].astype(jnp.float32)
                        + from_core[before, chip, span(hb)].astype(jnp.float32),
                    )
                    if j < chips:
                        rx(before, hb, j).start()

            @pl.when(u >= LAG)
            def _():
                forward(*unit(jnp.maximum(u - LAG, 0)))

        if last:
            bring_home()
        for u in range(units + 1 - LAG, units):
            forward(*unit(u))
        for h in range(halves):
            sums[...] = over_chips(z, h)
            for way in range(2):

                @pl.when(z > 0 if way == 0 else z < owners - 1)
                def _():
                    slot, copy = rz_from(z, h, way)
                    copy.wait_recv()
                    sums[...] += from_owner[slot, span(h)].astype(jnp.float32)

            mass = join_mass(sums[:, width:])
            renewed = (sums[:, :width] + PRIOR * cents[z, s, span(h)].astype(jnp.float32)) / (mass + PRIOR)
            if last:
                centre_out[span(h)] = renewed.astype(jnp.bfloat16)
            else:
                cents[z, s, span(h)] = renewed.astype(jnp.bfloat16)

    def bring_home():
        for b in range(blocks):
            o = owner_ref[cluster_ref[b]]
            rank = jnp.int32(0)
            for e in range(b):
                rank = rank + jnp.where(owner_ref[cluster_ref[e]] == o, jnp.int32(1), jnp.int32(0))
            weight_out[b] = wts[o * cap + rank].astype(jnp.float32).T.astype(jnp.bfloat16)

    def forward(o, h):
        for way in range(2):

            @pl.when(o > z if way == 0 else o < z)
            def _():
                total = over_chips(o, h)
                store_sum(o, x, h, total)

                @pl.when(z > 0 if way == 0 else z < owners - 1)
                def _():
                    slot, copy = rz_from(o, h, way)
                    copy.wait_recv()
                    store_sum(o, x, h, total + from_owner[slot, span(h)].astype(jnp.float32))

                rz(o, h, way).start()

    def reduce_done():
        @pl.loop(0, owners)
        def _(o):
            rc(o).wait_send()
            for h in range(halves):
                for j in range(1, chips):
                    rx(o, h, j).wait_send()

                @pl.when(o > z)
                def _():
                    rz(o, h, 0).wait_send()

                @pl.when(o < z)
                def _():
                    rz(o, h, 1).wait_send()

    for sweep in range(ITERS):
        gather(sweep == 0)
        if sweep == 0:
            load_rows.wait()
        else:
            reduce_done()
        reduce(sweep == ITERS - 1)
    reduce_done()


def body(embeddings, subcentroids, block_cluster, owner_map):
    owners = lax.axis_size("dp")
    parts = lax.axis_size("split")
    chips = parts // 2
    blocks = block_cluster.shape[0]
    total_rows, width = embeddings.shape
    block_rows = total_rows // blocks
    cap = max(2, 2 * blocks // owners)
    subs = subcentroids.shape[1]
    portion = subs // parts
    wide = width + LANES
    bf16 = jnp.bfloat16
    sems = pltpu.SemaphoreType.DMA
    flops = 2 * ITERS * subs * width * block_rows * (blocks + owners * cap)
    weights, centres = pl.pallas_call(
        functools.partial(kernel, owners, chips, cap),
        out_shape=(
            jax.ShapeDtypeStruct((blocks, block_rows, subs), bf16),
            jax.ShapeDtypeStruct((portion, width), bf16),
        ),
        in_specs=[
            pl.BlockSpec(memory_space=pltpu.SMEM),
            pl.BlockSpec(memory_space=pltpu.SMEM),
            pl.BlockSpec(memory_space=pl.ANY),
            pl.BlockSpec(memory_space=pl.ANY),
        ],
        out_specs=(
            pl.BlockSpec(memory_space=pltpu.VMEM),
            pl.BlockSpec(memory_space=pltpu.VMEM),
        ),
        scratch_shapes=[
            pltpu.VMEM((blocks, block_rows, width), bf16),
            pltpu.VMEM((owners, parts, portion, width), bf16),
            pltpu.VMEM((owners * cap, subs, block_rows), bf16),
            pltpu.VMEM((subs, cap * block_rows), bf16),
            pltpu.VMEM((owners, 2, chips, portion, wide), bf16),
            pltpu.VMEM((owners, chips, portion, wide), bf16),
            pltpu.VMEM((owners, max(1, chips - 1), portion, wide), bf16),
            pltpu.VMEM((owners + 1, portion, wide), bf16),
            pltpu.VMEM((portion // (2 if portion % 32 == 0 else 1), wide), jnp.float32),
            sems((2,)),
            sems((owners, 2, 2)), sems((owners, 2)),
            sems((owners, 2, chips)), sems((owners, 2, chips)),
            sems((owners, 2, chips)), sems((owners, 2, chips)),
            sems((owners,)), sems((owners,)),
            sems((owners, 2, chips)), sems((owners, 2, chips)),
            sems((owners, 2)), sems((owners + 1, 2)),
        ],
        compiler_params=pltpu.CompilerParams(
            collective_id=0, has_side_effects=True, vmem_limit_bytes=58 * 1024 * 1024
        ),
        cost_estimate=pl.CostEstimate(
            flops=flops, bytes_accessed=2 * total_rows * width, transcendentals=total_rows * subs
        ),
    )(
        block_cluster, owner_map,
        embeddings.reshape(blocks, block_rows, width),
        subcentroids.reshape(parts, portion, width),
    )
    return weights.reshape(total_rows, subs), centres[None]


def solution(mesh):
    return jax.shard_map(
        body,
        mesh=mesh,
        in_specs=(
            P(("groups", "dp", "split"), None),
            P(("groups", "dp"), None, None),
            P(("groups", "dp", "split")),
            P("groups"),
        ),
        out_specs=(P(("groups", "dp", "split"), None), P(("groups", "dp"), "split", None)),
        check_vma=False,
    )
```

```python
import functools

import jax
import jax.numpy as jnp
from jax import lax
from jax.experimental import pallas as pl
from jax.experimental.pallas import tpu as pltpu
from jax.sharding import PartitionSpec as P

MESH = pl.DeviceIdType.MESH
ITERS = 2
PRIOR = 4.0
LANES = 128
LAG = 4


def split_mass(mass):
    high = mass.astype(jnp.bfloat16).astype(jnp.float32)
    lane = lax.broadcasted_iota(jnp.int32, (mass.shape[0], LANES), 1)
    return jnp.where(lane < LANES // 2, high, mass - high).astype(jnp.bfloat16)


def join_mass(pair):
    return pair[:, :1] + pair[:, LANES // 2 : LANES // 2 + 1]


def kernel(
    owners, chips, cap,
    cluster_ref, owner_ref, rows_hbm, sub_hbm,
    weight_out, centre_out,
    rows, cents, wts, wcat, part, from_core, from_chip, from_owner, sums,
    load_sem, gz_send, gz_recv, gx_send, gx_recv, gc_send, gc_recv,
    rc_send, rc_recv, rx_send, rx_recv, rz_send, rz_recv,
):
    blocks, block_rows, width = rows.shape
    parts, portion = cents.shape[1], cents.shape[2]
    subs = parts * portion
    inv_root = width ** (-0.5)
    z = lax.axis_index("dp")
    s = lax.axis_index("split")
    x = lax.div(s, 2)
    c = s - 2 * x
    sibling = 2 * x + (1 - c)
    halves = 2 if portion % 32 == 0 else 1
    rows_half = portion // halves

    def span(h):
        return pl.ds(pl.multiple_of(h * rows_half, rows_half), rows_half)

    def chip_at(j):
        return lax.rem(x + j, chips)

    def remote(src, dst, send, recv, axis, index):
        return pltpu.make_async_remote_copy(
            src_ref=src, dst_ref=dst, send_sem=send, recv_sem=recv,
            device_id={axis: index}, device_id_type=MESH,
        )

    load_rows = pltpu.make_async_copy(rows_hbm, rows, load_sem.at[0])
    load_sub = pltpu.make_async_copy(sub_hbm, cents.at[z], load_sem.at[1])
    load_sub.start()
    load_rows.start()

    barrier = pltpu.get_barrier_semaphore()
    pl.semaphore_signal(barrier, inc=1, device_id={"split": sibling}, device_id_type=MESH)
    for j in range(1, chips):
        pl.semaphore_signal(barrier, inc=1, device_id={"split": 2 * chip_at(j) + c}, device_id_type=MESH)
    for way in range(2):

        @pl.when(z < owners - 1 if way == 0 else z > 0)
        def _():
            pl.semaphore_signal(barrier, inc=1, device_id={"dp": z + 1 - 2 * way}, device_id_type=MESH)

    links = jnp.where(z > 0, 1, 0) + jnp.where(z < owners - 1, 1, 0)
    pl.semaphore_wait(barrier, chips + links)
    load_sub.wait()

    def gz(o, h, way):
        ref = cents.at[o, s, span(h)]
        return remote(ref, ref, gz_send.at[o, h, way], gz_recv.at[o, h], "dp", z + 1 - 2 * way)

    def gz_from(o, h, way):
        ref = cents.at[o, s, span(h)]
        return remote(ref, ref, gz_send.at[o, h, way], gz_recv.at[o, h], "dp", z - 1 + 2 * way)

    def has_next(way):
        return z < owners - 1 if way == 0 else z > 0

    def gx(o, h, j):
        ref = cents.at[o, s, span(h)]
        return remote(ref, ref, gx_send.at[o, h, j], gx_recv.at[o, h, x], "split", 2 * chip_at(j) + c)

    def gx_from(o, h, j):
        ref = cents.at[o, 2 * chip_at(j) + c, span(h)]
        return remote(ref, ref, gx_send.at[o, h, j], gx_recv.at[o, h, chip_at(j)], "split", 2 * chip_at(j) + c)

    def gc(o, h, chip):
        ref = cents.at[o, 2 * chip + c, span(h)]
        return remote(ref, ref, gc_send.at[o, h, chip], gc_recv.at[o, h, chip], "split", sibling)

    def gc_from(o, h, chip):
        ref = cents.at[o, 2 * chip + 1 - c, span(h)]
        return remote(ref, ref, gc_send.at[o, h, chip], gc_recv.at[o, h, chip], "split", sibling)

    def spread(o, h):
        for j in range(1, chips):
            gx(o, h, j).start()
        gc(o, h, x).start()

    def pass_on(o, h):
        for j in range(1, chips):
            gx_from(o, h, j).wait_recv()
            gc(o, h, chip_at(j)).start()

    def settle(o):
        for h in range(halves):
            for chip in range(chips):
                gc_from(o, h, chip).wait_recv()
                gc(o, h, chip).wait_send()
            for j in range(1, chips):
                gx(o, h, j).wait_send()

    def at_distance(k, act):
        for way in range(2):
            o = z - k if way == 0 else z + k

            @pl.when(o >= 0 if way == 0 else o < owners)
            def _():
                act(o, way)

    def onward(o, h, way, done):
        @pl.when(has_next(way))
        def _():
            if done:
                gz(o, h, way).wait_send()
            else:
                gz(o, h, way).start()

    def gather(first):
        if first:
            for h in range(halves):
                for way in range(2):
                    onward(z, h, way, False)

        @pl.loop(1, owners + 1)
        def _(k):
            for h in range(halves):

                def arrive(o, way, h=h):
                    gz_from(o, h, way).wait_recv()
                    onward(o, h, way, False)
                    spread(o, h)

                at_distance(k, arrive)

                @pl.when(k > 1)
                def _():
                    at_distance(k - 1, lambda o, way, h=h: pass_on(o, h))

                if not first:

                    @pl.when(k == 1)
                    def _():
                        pass_on(z, h)

        def finish(o, way):
            for h in range(halves):
                onward(o, h, way, True)
            settle(o)

        for h in range(halves):
            for way in range(2):
                onward(z, h, way, True)
        if not first:
            settle(z)

        @pl.loop(1, owners)
        def _(k):
            at_distance(k, finish)

    def rc(o):
        return remote(part.at[o, 1 - c], from_core.at[o], rc_send.at[o], rc_recv.at[o], "split", sibling)

    def rx(o, h, j):
        return remote(
            part.at[o, c, chip_at(j), span(h)], from_chip.at[o, j - 1, span(h)],
            rx_send.at[o, h, j], rx_recv.at[o, h, j], "split", 2 * chip_at(j) + c,
        )

    def rz(o, h, way):
        slot = o if way == 0 else jnp.where(o == z - 1, owners, o)
        return remote(
            part.at[o, c, x, span(h)], from_owner.at[slot, span(h)],
            rz_send.at[o, h], rz_recv.at[slot, h], "dp", z + 1 - 2 * way,
        )

    def rz_from(o, h, way):
        slot = o if way == 0 else jnp.where(o == z, owners, o)
        return slot, remote(
            part.at[o, c, x, span(h)], from_owner.at[slot, span(h)],
            rz_send.at[o, h], rz_recv.at[slot, h], "dp", z - 1 + 2 * way,
        )

    below, above = z, owners - 1 - z
    far = jnp.maximum(below, above)
    near = jnp.minimum(below, above)
    far_sign = jnp.where(above >= below, 1, -1)

    def farthest(t):
        u = t - (far - near)
        half = lax.div(jnp.maximum(u, 0), 2)
        sign = jnp.where(u - 2 * half == 1, -far_sign, far_sign)
        return jnp.where(u < 0, z + far_sign * (far - t), z + sign * (near - half))

    def weigh(o, last):
        ids = [jnp.int32(0)] * cap
        live = [jnp.int32(0)] * cap
        count = jnp.int32(0)
        for b in range(blocks):
            hit = jnp.where(owner_ref[cluster_ref[b]] == o, jnp.int32(1), jnp.int32(0))
            for j in range(cap):
                take = hit * jnp.where(count == j, jnp.int32(1), jnp.int32(0))
                ids[j] = ids[j] + take * b
                live[j] = live[j] + take
            count = count + hit
        centre = cents[o].reshape(subs, width)
        held = centre.astype(jnp.float32)
        squares = jnp.sum(held * held, axis=1, keepdims=True)
        mass = jnp.zeros((subs, 1), jnp.float32)
        for j in range(cap):
            dots = lax.dot_general(
                centre, rows[ids[j]], (((1,), (1,)), ((), ())), preferred_element_type=jnp.float32
            )
            logits = (2.0 * dots - squares) * inv_root
            power = jnp.exp(logits - jnp.max(logits, axis=0, keepdims=True))
            weight = (power / jnp.sum(power, axis=0, keepdims=True)).astype(jnp.bfloat16)
            if last:
                wts[o * cap + j] = weight
            piece = weight.astype(jnp.float32) * live[j].astype(jnp.float32)
            wcat[:, j * block_rows : (j + 1) * block_rows] = piece.astype(jnp.bfloat16)
            mass = mass + jnp.sum(piece, axis=1, keepdims=True)
        mass = split_mass(mass)
        step = 512 if width % 512 == 0 else width
        weights = wcat[...]
        for n in range(width // step):
            cols = slice(n * step, (n + 1) * step)
            taken = jnp.concatenate([rows[ids[j], :, cols] for j in range(cap)], axis=0)
            product = jnp.dot(weights, taken, preferred_element_type=jnp.float32).astype(jnp.bfloat16)
            for q in range(parts):
                part[o, q % 2, q // 2, :, cols] = product[q * portion : (q + 1) * portion]
        for q in range(parts):
            part[o, q % 2, q // 2, :, width:] = mass[q * portion : (q + 1) * portion]

    def store_sum(o, chip, h, total):
        part[o, c, chip, span(h), :width] = total[:, :width].astype(jnp.bfloat16)
        part[o, c, chip, span(h), width:] = split_mass(join_mass(total[:, width:]))

    def over_chips(o, h):
        total = part[o, c, x, span(h)].astype(jnp.float32)
        for j in range(1, chips):
            rx(o, h, chips - j).wait_recv()
            total = total + from_chip[o, chips - j - 1, span(h)].astype(jnp.float32)
        return total

    def reduce(last):
        units = owners * halves

        def unit(u):
            t = lax.div(u, halves)
            return farthest(t), u - t * halves

        @pl.loop(0, units + 1)
        def _(u):
            o, h = unit(u)

            @pl.when((u < units) & (h == 0))
            def _():
                weigh(o, last)
                rc(o).start()

            before, hb = unit(jnp.maximum(u - 1, 0))

            @pl.when(u >= 1)
            def _():
                @pl.when(hb == 0)
                def _():
                    rc(before).wait_recv()

                for j in range(1, chips + 1):
                    chip = chip_at(j)
                    store_sum(
                        before, chip, hb,
                        part[before, c, chip, span(hb)].astype(jnp.float32)
                        + from_core[before, chip, span(hb)].astype(jnp.float32),
                    )
                    if j < chips:
                        rx(before, hb, j).start()

            @pl.when(u >= LAG)
            def _():
                forward(*unit(jnp.maximum(u - LAG, 0)))

        if last:
            bring_home()
        for u in range(units + 1 - LAG, units):
            forward(*unit(u))
        for h in range(halves):
            sums[...] = over_chips(z, h)
            for way in range(2):

                @pl.when(z > 0 if way == 0 else z < owners - 1)
                def _():
                    slot, copy = rz_from(z, h, way)
                    copy.wait_recv()
                    sums[...] += from_owner[slot, span(h)].astype(jnp.float32)

            mass = join_mass(sums[:, width:])
            renewed = (sums[:, :width] + PRIOR * cents[z, s, span(h)].astype(jnp.float32)) / (mass + PRIOR)
            if last:
                centre_out[span(h)] = renewed.astype(jnp.bfloat16)
            else:
                cents[z, s, span(h)] = renewed.astype(jnp.bfloat16)
                for way in range(2):
                    onward(z, h, way, False)
                spread(z, h)

    def bring_home():
        for b in range(blocks):
            o = owner_ref[cluster_ref[b]]
            rank = jnp.int32(0)
            for e in range(b):
                rank = rank + jnp.where(owner_ref[cluster_ref[e]] == o, jnp.int32(1), jnp.int32(0))
            weight_out[b] = wts[o * cap + rank].astype(jnp.float32).T.astype(jnp.bfloat16)

    def forward(o, h):
        for way in range(2):

            @pl.when(o > z if way == 0 else o < z)
            def _():
                total = over_chips(o, h)
                store_sum(o, x, h, total)

                @pl.when(z > 0 if way == 0 else z < owners - 1)
                def _():
                    slot, copy = rz_from(o, h, way)
                    copy.wait_recv()
                    store_sum(o, x, h, total + from_owner[slot, span(h)].astype(jnp.float32))

                rz(o, h, way).start()

    def reduce_done():
        @pl.loop(0, owners)
        def _(o):
            rc(o).wait_send()
            for h in range(halves):
                for j in range(1, chips):
                    rx(o, h, j).wait_send()

                @pl.when(o > z)
                def _():
                    rz(o, h, 0).wait_send()

                @pl.when(o < z)
                def _():
                    rz(o, h, 1).wait_send()

    for sweep in range(ITERS):
        gather(sweep == 0)
        if sweep == 0:
            load_rows.wait()
        else:
            reduce_done()
        reduce(sweep == ITERS - 1)
    reduce_done()


def body(embeddings, subcentroids, block_cluster, owner_map):
    owners = lax.axis_size("dp")
    parts = lax.axis_size("split")
    chips = parts // 2
    blocks = block_cluster.shape[0]
    total_rows, width = embeddings.shape
    block_rows = total_rows // blocks
    cap = max(2, 2 * blocks // owners)
    subs = subcentroids.shape[1]
    portion = subs // parts
    wide = width + LANES
    bf16 = jnp.bfloat16
    sems = pltpu.SemaphoreType.DMA
    flops = 2 * ITERS * subs * width * block_rows * (blocks + owners * cap)
    weights, centres = pl.pallas_call(
        functools.partial(kernel, owners, chips, cap),
        out_shape=(
            jax.ShapeDtypeStruct((blocks, block_rows, subs), bf16),
            jax.ShapeDtypeStruct((portion, width), bf16),
        ),
        in_specs=[
            pl.BlockSpec(memory_space=pltpu.SMEM),
            pl.BlockSpec(memory_space=pltpu.SMEM),
            pl.BlockSpec(memory_space=pl.ANY),
            pl.BlockSpec(memory_space=pl.ANY),
        ],
        out_specs=(
            pl.BlockSpec(memory_space=pltpu.VMEM),
            pl.BlockSpec(memory_space=pltpu.VMEM),
        ),
        scratch_shapes=[
            pltpu.VMEM((blocks, block_rows, width), bf16),
            pltpu.VMEM((owners, parts, portion, width), bf16),
            pltpu.VMEM((owners * cap, subs, block_rows), bf16),
            pltpu.VMEM((subs, cap * block_rows), bf16),
            pltpu.VMEM((owners, 2, chips, portion, wide), bf16),
            pltpu.VMEM((owners, chips, portion, wide), bf16),
            pltpu.VMEM((owners, max(1, chips - 1), portion, wide), bf16),
            pltpu.VMEM((owners + 1, portion, wide), bf16),
            pltpu.VMEM((portion // (2 if portion % 32 == 0 else 1), wide), jnp.float32),
            sems((2,)),
            sems((owners, 2, 2)), sems((owners, 2)),
            sems((owners, 2, chips)), sems((owners, 2, chips)),
            sems((owners, 2, chips)), sems((owners, 2, chips)),
            sems((owners,)), sems((owners,)),
            sems((owners, 2, chips)), sems((owners, 2, chips)),
            sems((owners, 2)), sems((owners + 1, 2)),
        ],
        compiler_params=pltpu.CompilerParams(
            collective_id=0, has_side_effects=True, vmem_limit_bytes=58 * 1024 * 1024
        ),
        cost_estimate=pl.CostEstimate(
            flops=flops, bytes_accessed=2 * total_rows * width, transcendentals=total_rows * subs
        ),
    )(
        block_cluster, owner_map,
        embeddings.reshape(blocks, block_rows, width),
        subcentroids.reshape(parts, portion, width),
    )
    return weights.reshape(total_rows, subs), centres[None]


def solution(mesh):
    return jax.shard_map(
        body,
        mesh=mesh,
        in_specs=(
            P(("groups", "dp", "split"), None),
            P(("groups", "dp"), None, None),
            P(("groups", "dp", "split")),
            P("groups"),
        ),
        out_specs=(P(("groups", "dp", "split"), None), P(("groups", "dp"), "split", None)),
        check_vma=False,
    )
```
